256 devices in a mesh: tm: 32 (over y, z_hi, core), batch: 8 (over x, z_lo).
Axes of the slice: x: 4, y: 4, z: 8 (z_hi: 4, z_lo: 2; z = z_hi * 2 + z_lo), core: 2. Of those that a mesh axis runs over, the one named last changes fastest.
Arguments:
- features: bfloat16 [8, 2048, 128, 128], P('batch', 'tm'), may hold values from -6 to 6
- kernel_one: bfloat16 [3, 3, 128, 128], replicated, may hold values from -0.1875 to 0.1875
- proj_weight: bfloat16 [512, 1024], P(None, 'tm'), may hold values from -0.25 to 0.25
- upstream: bfloat16 [8, 1024, 64, 1024], P('batch', 'tm'), may hold values from -6 to 6
Outputs:
- projected: bfloat16 [8, 1024, 64, 1024], P('batch', 'tm')
- grad_features: bfloat16 [8, 2048, 128, 128], P('batch', 'tm')
- grad_kernel_one: float32 [3, 3, 128, 128], replicated
- grad_proj: float32 [512, 1024], P(None, 'tm')
The draws below stay inside these ranges and needn't reach their ends.
All inputs are finite; a program needn't handle non-finite values.
Results may differ from the reference program's by a relative error of at most 0.0049.
Values may be sent and summed in bfloat16 or wider, within the bound.
A program may use at most 128 MiB of HBM per device.

```python
import math
import jax
import jax.numpy as jnp
from jax import lax

MEL = 128
CHAN = 128
FILT = 1024
DEPTH = 512
BATCH = 8
FRAMES = 2048


def shard_levels(own_key, extent, pieces, least, top_value):
    factor_of, own = 1.0, jax.random.fold_in(own_key, 6)
    for dim, shards_of in pieces:
        steps = jnp.exp(jax.random.uniform(jax.random.fold_in(own, dim), (shards_of,), jnp.float32, least / len(pieces), top_value / len(pieces)))
        factor_of = factor_of * jnp.repeat(steps, extent[dim] // shards_of).reshape([-1 if axis == dim else 1 for axis in range(len(extent))])
    return factor_of


def gaussian(stream_key, dims, spread, limit, split=(), dtype=jnp.bfloat16):
    level = shard_levels(stream_key, dims, split, -0.22, 0.18) if split else 1.0
    array = jax.random.normal(stream_key, dims, jnp.float32) * spread * level
    return jnp.minimum(jnp.maximum(array, -limit), limit).astype(dtype)


def setup_inputs(seed: int = 0) -> dict:
    key_list = jax.random.split(jax.random.key(seed), 5)
    return {
        "features": gaussian(key_list[0], (BATCH, FRAMES, MEL, CHAN), 1.0, 6.0, ((0, 8), (1, 32))),
        "kernel_one": gaussian(key_list[1], (3, 3, CHAN, CHAN), (9 * CHAN) ** -0.5, 0.1875),
        "proj_weight": gaussian(key_list[2], (DEPTH, FILT), DEPTH ** -0.5, 0.25, ((1, 32),)),
        "upstream": gaussian(key_list[3], (BATCH, FRAMES // 2, MEL // 2, FILT), 1.0, 6.0, ((0, 8), (1, 32))),
    }


def conv_same(values, kernel):
    return lax.conv_general_dilated(values.astype(jnp.float32), kernel.astype(jnp.float32), (1, 1), ((1, 1), (1, 1)), dimension_numbers=('NHWC', 'HWIO', 'NHWC'), precision=lax.Precision.HIGHEST)

def flipped(kernel):
    return jnp.transpose(jnp.flip(kernel, (0, 1)), (0, 1, 3, 2))

def silu_slope(values):
    sig = jax.nn.sigmoid(values)
    return sig * (1.0 + values * (1.0 - sig))

def kernel_grad(values, grad):
    batch_rows, frames, mels, chans = values.shape
    padded = jnp.pad(values, ((0, 0), (1, 1), (1, 1), (0, 0)))
    flat_grad = grad.reshape(-1, chans)
    rows_out = []
    for i in range(3):
        cols_out = []
        for j in range(3):
            piece = padded[:, i:i + frames, j:j + mels, :].reshape(-1, chans)
            cols_out.append(jnp.dot(piece.T, flat_grad, preferred_element_type=jnp.float32))
        rows_out.append(jnp.stack(cols_out))
    return jnp.stack(rows_out)

def reference(features, kernel_one, proj_weight, upstream):
    batch_rows, frames, mels, chans = features.shape
    filters = proj_weight.shape[1]
    scale = 1.0 / math.sqrt(batch_rows * frames * mels)
    pre_one = conv_same(features, kernel_one)
    hidden_two = (features.astype(jnp.float32) + jax.nn.silu(pre_one)).astype(jnp.bfloat16)
    packed = hidden_two.reshape(batch_rows, frames // 2, 2, mels // 2, 2, chans).transpose(0, 1, 3, 2, 4, 5).reshape(-1, 4 * chans)
    projected = jnp.dot(packed, proj_weight, preferred_element_type=jnp.float32).astype(jnp.bfloat16)
    cotangent = upstream.reshape(-1, filters)
    grad_packed = jnp.dot(cotangent, proj_weight.T, preferred_element_type=jnp.float32)
    grad_hidden_two = grad_packed.reshape(batch_rows, frames // 2, mels // 2, 2, 2, chans).transpose(0, 1, 3, 2, 4, 5).reshape(batch_rows, frames, mels, chans)
    grad_pre_one = (grad_hidden_two * silu_slope(pre_one)).astype(jnp.bfloat16)
    grad_features = (grad_hidden_two + conv_same(grad_pre_one, flipped(kernel_one))).astype(jnp.bfloat16)
    grad_kernel_one = kernel_grad(features, grad_pre_one) * scale
    grad_proj = jnp.dot(packed.T, cotangent, preferred_element_type=jnp.float32) * scale
    return (projected.reshape(upstream.shape), grad_features, grad_kernel_one, grad_proj)
```

```python
import math

import jax
import jax.numpy as jnp
from jax import lax
from jax.experimental import pallas as pl
from jax.experimental.pallas import tpu as pltpu
from jax.sharding import PartitionSpec as P

BF = jnp.bfloat16
F32 = jnp.float32
MESH = pl.DeviceIdType.MESH


def dot(a, b):
    return jnp.dot(a, b, preferred_element_type=F32)


def place(dst, i, block):
    base = i * 512
    zero = jnp.zeros((128, 128), BF)
    dst[base : base + 128, 0:128] = block(1)
    dst[base : base + 128, 128:256] = block(0)
    dst[base + 128 : base + 256, 0:128] = block(2)
    dst[base + 128 : base + 256, 128:256] = block(1)
    dst[base + 256 : base + 384, 0:128] = block(0)
    dst[base + 256 : base + 384, 128:256] = zero
    dst[base + 384 : base + 512, 0:128] = zero
    dst[base + 384 : base + 512, 128:256] = block(2)


def kernel(
    scale, feat, kern, pw, up, proj_out, gf_out, gk_out, gp_out,
    fx, st, x4, y4, sl, pk, pkt, gh, ub, wt, wn, wf, wb, po, gfo, gt, dk,
    gps, r0, s1, r1, s2, r2, s3, r3,
    k0, ra, sb, rb, sc, rc, kd, ke,
    in_sem, pout_sem, fout_sem,
    hx_s, hx_r, hy_s, hy_r, wz_s, wz_r, wy_s, wy_r, wc_s, wc_r,
    g0_s, g0_r, g1_s, g1_r, g2_s, g2_r, g3_s, g3_r,
    ka_s, ka_r, kb_s, kb_r, kc_s, kc_r, kd_s, kd_r, ke_s, ke_r,
):
    tm = lax.axis_index("tm")
    bt = lax.axis_index("batch")
    core, zh, y = tm % 2, (tm // 2) % 4, tm // 8
    x, zl = bt // 2, bt % 2
    z = zh * 2 + zl
    xy = x * 4 + y

    def device(cx, cy, cz, cc):
        return {"tm": (cy * 4 + cz // 2) * 2 + cc, "batch": cx * 2 + cz % 2}

    def remote(src, dst, ssem, rsem, dev):
        return pltpu.make_async_remote_copy(
            src_ref=src, dst_ref=dst, send_sem=ssem, recv_sem=rsem,
            device_id=dev, device_id_type=MESH,
        )

    partner = device(x, y, z, 1 - core)
    left = {"tm": (tm + 31) % 32, "batch": bt}
    right = {"tm": (tm + 1) % 32, "batch": bt}

    def y_peer(d):
        return device(x, (y + d) % 4, z, core)

    def z_peer(d):
        return device(x, y, (z + d) % 8, core)

    def b_peer(d):
        return {"tm": tm, "batch": (bt + d) % 8}

    def xy_peer(d):
        return device((x + d // 4) % 4, (y + d % 4) % 4, z, core)

    feat_in = pltpu.make_async_copy(feat, fx, in_sem.at[0])
    up_in = pltpu.make_async_copy(up, ub, in_sem.at[1])
    feat_in.start()
    up_in.start()

    barrier = pltpu.get_barrier_semaphore()
    greet = [partner, left, right]
    greet += [z_peer(d) for d in range(1, 8)]
    greet += [b_peer(d) for d in range(1, 8)]
    greet += [xy_peer(d) for d in range(1, 16)]
    for dev in greet:
        pl.semaphore_signal(barrier, inc=1, device_id=dev, device_id_type=MESH)

    wt[y, zh, core] = pw[...].T
    for i in range(3):
        place(wf, i, lambda j: kern[i, j])
        place(wb, i, lambda j: kern[2 - i, 2 - j].T)

    row = lax.broadcasted_iota(jnp.int32, (512, 128), 0) % 64

    def build(k):
        st[8:1032, :] = fx[pl.ds(k * 8, 8)].reshape(1024, 128).astype(F32)
        at = pl.ds(k * 8 + 1, 8)
        x4[at, :, 0:128] = st[pl.ds(8, 512, stride=2), :].astype(BF).reshape(8, 64, 128)
        x4[at, :, 128:256] = st[pl.ds(9, 512, stride=2), :].astype(BF).reshape(8, 64, 128)
        low = jnp.where(row == 0, 0.0, st[pl.ds(7, 512, stride=2), :])
        x4[at, :, 256:384] = low.astype(BF).reshape(8, 64, 128)
        high = jnp.where(row == 63, 0.0, st[pl.ds(10, 512, stride=2), :])
        x4[at, :, 384:512] = high.astype(BF).reshape(8, 64, 128)

    feat_in.wait()
    build(0)
    build(7)

    pl.semaphore_wait(barrier, len(greet))

    side = 2 * zl - 1
    wz = [
        remote(
            wt.at[y, zh, core], wt.at[y, zh, core], wz_s.at[d - 1], wz_r.at[d - 1],
            device(x, y, (z + side * d + 8) % 8, core),
        )
        for d in range(1, 4)
    ]
    for copy in wz:
        copy.start()
    hx = [
        remote(x4.at[1], x4.at[65], hx_s.at[0], hx_r.at[0], left),
        remote(x4.at[64], x4.at[0], hx_s.at[1], hx_r.at[1], right),
    ]
    for copy in hx:
        copy.start()

    @pl.loop(1, 7)
    def _(k):
        build(k)

    def forward(k):
        t0 = k * 8
        lhs = jnp.concatenate([x4[pl.ds(t0 + i, 8)].reshape(512, 512) for i in range(3)], axis=1)
        pre = dot(lhs, wf[...])
        here = x4[pl.ds(t0 + 1, 8), :, 0:256].reshape(512, 256).astype(F32)
        sig = 0.5 * jnp.tanh(0.5 * pre) + 0.5
        act = pre * sig
        slope = (sig + act * (1.0 - sig)).reshape(4, 2, 64, 256)
        hidden = (here + act).astype(BF).reshape(4, 2, 64, 256)
        at = pl.ds(k * 4, 4)
        both = jnp.concatenate([hidden[:, 0], hidden[:, 1]], axis=-1)
        pk[at] = both
        sl[at, :, 0:256] = slope[:, 0]
        sl[at, :, 256:512] = slope[:, 1]
        pkt[:, pl.ds(pl.multiple_of(k * 256, 256), 256)] = both.reshape(256, 512).T

    @pl.loop(1, 4)
    def _(k):
        forward(k)

    for copy in wz:
        copy.wait()
    wy = [
        remote(wt.at[y, :, core], wt.at[y, :, core], wy_s.at[d - 1], wy_r.at[d - 1], y_peer(d))
        for d in range(1, 4)
    ]
    wc = [
        remote(
            wt.at[(y + 4 - d) % 4, :, core], wt.at[(y + 4 - d) % 4, :, core],
            wc_s.at[d], wc_r.at[d], partner,
        )
        for d in range(4)
    ]
    for copy in wy:
        copy.start()
    wc[0].start()

    @pl.loop(4, 7)
    def _(k):
        forward(k)

    for copy in hx:
        copy.wait()

    @pl.when(tm == 0)
    def _():
        x4[0] = jnp.zeros((64, 512), BF)

    @pl.when(tm == 31)
    def _():
        x4[65] = jnp.zeros((64, 512), BF)

    forward(0)
    forward(7)

    up_in.wait()
    order = [2, 1, 3, 0]
    g0 = {
        d: remote(
            gps.at[(y + d) % 4, :, 1 - core], r0.at[(y + d) % 4], g0_s.at[d], g0_r.at[d], partner
        )
        for d in order
    }
    g1 = {
        d: remote(s1.at[(y + d) % 4], r1.at[y], g1_s.at[d - 1], g1_r.at[d - 1], y_peer(d))
        for d in (1, 2, 3)
    }

    def proj_chunk(d):
        cols = pl.ds(pl.multiple_of(((y + d) % 4) * 256, 256), 256)
        part = dot(pkt[...], ub[:, :, cols].reshape(2048, 256))
        gps[(y + d) % 4] = part.astype(BF).T.reshape(4, 2, 32, 512)
        g0[d].start()

    def core_sum(d):
        g0[d].wait()
        yd = (y + d) % 4
        total = gps[yd, :, core].astype(F32) + r0[yd].astype(F32)
        if d == 0:
            r1[y] = total.astype(BF)
        else:
            s1[yd] = total.astype(BF)
            g1[d].start()

    def pass_on(d):
        wy[d - 1].wait()
        wc[d].start()

    proj_chunk(2)
    pass_on(1)
    proj_chunk(1)
    core_sum(2)
    pass_on(3)
    proj_chunk(3)
    core_sum(1)
    pass_on(2)
    proj_chunk(0)
    core_sum(3)

    for copy in wc:
        copy.wait()

    for yy in range(4):
        wn[:, yy * 256 : (yy + 1) * 256] = wt[yy].reshape(256, 512).T

    row3 = lax.broadcasted_iota(jnp.int32, (8, 64, 128), 1)

    def grads(k):
        at = pl.ds(k * 8, 8)
        gp = dot(ub[at].reshape(512, 1024), wt[...].reshape(1024, 512))
        gh[at] = gp.reshape(8, 64, 512)
        g = (gp * sl[at].reshape(512, 512)).astype(BF).reshape(8, 64, 512)
        gf = g.astype(F32)
        lows, highs = [], []
        for p in range(2):
            odd = gf[:, :, p * 256 + 128 : p * 256 + 256]
            even = gf[:, :, p * 256 : p * 256 + 128]
            lows.append(jnp.where(row3 == 0, 0.0, pltpu.roll(odd, 1, 1)).astype(BF))
            highs.append(jnp.where(row3 == 63, 0.0, pltpu.roll(even, 63, 1)).astype(BF))
        for t in range(8):
            for p in range(2):
                f = k * 16 + 1 + 2 * t + p
                y4[f, :, 0:256] = g[t, :, p * 256 : p * 256 + 256]
                y4[f, :, 256:384] = lows[p][t]
                y4[f, :, 384:512] = highs[p][t]
        rows = jnp.concatenate(
            [g[t, :, p * 256 : p * 256 + 256] for t in range(8) for p in range(2)], axis=0
        )
        gt[:, pl.ds(pl.multiple_of(k * 1024, 1024), 1024)] = rows.T

    grads(0)
    grads(3)
    hy = [
        remote(y4.at[1], y4.at[65], hy_s.at[0], hy_r.at[0], left),
        remote(y4.at[64], y4.at[0], hy_s.at[1], hy_r.at[1], right),
    ]
    for copy in hy:
        copy.start()
    core_sum(0)

    @pl.loop(1, 3)
    def _(k):
        grads(k)

    for copy in g1.values():
        copy.wait()
    total = r1[0].astype(F32)
    for yy in range(1, 4):
        total = total + r1[yy].astype(F32)
    s2[...] = total.astype(BF).reshape(4, 2, 16, 512)
    g2 = []
    for d in range(1, 8):
        zd = (z + d) % 8
        g2.append(remote(s2.at[zd // 2, zd % 2], r2.at[z], g2_s.at[d - 1], g2_r.at[d - 1], z_peer(d)))
    for copy in g2:
        copy.start()
    r2[z] = s2[zh, zl]

    @pl.loop(0, 3)
    def _(i):
        dk[i] = dot(gt[...], x4[pl.ds(i, 64)].reshape(4096, 512))

    for i in range(3):
        q0, q1 = dk[i, 0:128], dk[i, 128:256]
        parts = (
            q1[:, 0:128] + q0[:, 256:384],
            q0[:, 0:128] + q1[:, 128:256],
            q0[:, 128:256] + q1[:, 384:512],
        )
        for j in range(3):
            block = parts[j].astype(BF).reshape(8, 16, 128)
            n = (i * 3 + j) * 8
            if n < 36 < n + 8:
                k0[0, n:36] = block[: 36 - n]
                k0[1, 0 : n - 28] = block[36 - n :]
            else:
                k0[n // 36, n % 36 : n % 36 + 8] = block
    ka = remote(k0.at[1 - core], ra, ka_s.at[0], ka_r.at[0], partner)
    ka.start()

    for copy in g2:
        copy.wait()
    total = r2[0].astype(F32)
    for zz in range(1, 8):
        total = total + r2[zz].astype(F32)
    s3[...] = total.astype(BF)
    g3 = [remote(s3, r3.at[bt], g3_s.at[d - 1], g3_r.at[d - 1], b_peer(d)) for d in range(1, 8)]
    for copy in g3:
        copy.start()
    r3[bt] = s3[...]

    def backward(k):
        t0 = k * 8
        lhs = jnp.concatenate([y4[pl.ds(t0 + i, 8)].reshape(512, 512) for i in range(3)], axis=1)
        out = dot(lhs, wb[...])
        h = gh[pl.ds(k * 4, 4)]
        out = out + jnp.concatenate(
            [h[t, :, p * 256 : p * 256 + 256] for t in range(4) for p in range(2)], axis=0
        )
        st[pl.ds(8, 512, stride=2), :] = out[:, 0:128]
        st[pl.ds(9, 512, stride=2), :] = out[:, 128:256]
        gfo[pl.ds(t0, 8)] = st[8:1032, :].astype(BF).reshape(8, 128, 128)
        pltpu.make_async_copy(gfo.at[pl.ds(t0, 8)], gf_out.at[pl.ds(t0, 8)], fout_sem.at[k]).start()

    def project(k):
        po[pl.ds(k * 8, 8)] = (
            dot(pk[pl.ds(k * 8, 8)].reshape(512, 512), wn[...]).astype(BF).reshape(8, 64, 1024)
        )
        pltpu.make_async_copy(po.at[pl.ds(k * 8, 8)], proj_out.at[pl.ds(k * 8, 8)], pout_sem.at[k]).start()

    @pl.loop(1, 3)
    def _(k):
        backward(k)

    ka.wait()
    sb[0:12] = (k0[core].astype(F32) + ra[...].astype(F32)).astype(BF).reshape(12, 3, 16, 128)
    sb[12:16] = jnp.zeros((4, 3, 16, 128), BF)
    kb = []
    for d in range(1, 16):
        owner = ((x + d // 4) % 4) * 4 + (y + d % 4) % 4
        kb.append(remote(sb.at[owner], rb.at[xy], kb_s.at[d - 1], kb_r.at[d - 1], xy_peer(d)))
    for copy in kb:
        copy.start()
    rb[xy] = sb[xy]

    @pl.loop(3, 6)
    def _(k):
        backward(k)

    for copy in kb:
        copy.wait()
    total = rb[0].astype(F32)
    for n in range(1, 16):
        total = total + rb[n].astype(F32)
    sc[...] = total.astype(BF)
    kc = [remote(sc, rc.at[z], kc_s.at[d - 1], kc_r.at[d - 1], z_peer(d)) for d in range(1, 8)]
    for copy in kc:
        copy.start()
    rc[z] = sc[...]

    for copy in hy:
        copy.wait()

    @pl.when(tm == 0)
    def _():
        y4[0] = jnp.zeros((64, 512), BF)

    @pl.when(tm == 31)
    def _():
        y4[65] = jnp.zeros((64, 512), BF)

    backward(0)

    @pl.loop(6, 8)
    def _(k):
        backward(k)

    for copy in kc:
        copy.wait()
    total = rc[0].astype(F32)
    for zz in range(1, 8):
        total = total + rc[zz].astype(F32)
    kd[xy] = total.astype(BF)
    kdc = [
        remote(kd.at[xy], kd.at[xy], kd_s.at[d - 1], kd_r.at[d - 1], xy_peer(d)) for d in range(1, 16)
    ]
    for copy in kdc:
        copy.start()

    @pl.loop(0, 2)
    def _(k):
        project(k)

    for copy in kdc:
        copy.wait()
    kec = remote(kd, ke, ke_s.at[0], ke_r.at[0], partner)
    kec.start()

    @pl.loop(2, 4)
    def _(k):
        project(k)

    for copy in g3:
        copy.wait()
    for half in range(2):
        total = r3[half].astype(F32)
        for n in range(1, 4):
            total = total + r3[2 * n + half].astype(F32)
        gp_out[half * 16 : half * 16 + 16, :] = total * scale

    kec.wait()
    gk_out[core] = kd[0:12].astype(F32).reshape(36, 16, 128) * scale
    gk_out[1 - core] = ke[0:12].astype(F32).reshape(36, 16, 128) * scale

    @pl.loop(0, 8)
    def _(k):
        pltpu.make_async_copy(gfo.at[pl.ds(k * 8, 8)], gf_out.at[pl.ds(k * 8, 8)], fout_sem.at[k]).wait()

    @pl.loop(0, 4)
    def _(k):
        pltpu.make_async_copy(po.at[pl.ds(k * 8, 8)], proj_out.at[pl.ds(k * 8, 8)], pout_sem.at[k]).wait()


def vm(*shape, dtype=BF):
    return pltpu.VMEM(shape, dtype)


def body(features, kernel_one, proj_weight, upstream):
    scale = 1.0 / math.sqrt(8 * 2048 * 128)
    dma = pltpu.SemaphoreType.DMA
    counts = [2, 4, 8]
    counts += [2, 2, 2, 2, 3, 3, 3, 3, 4, 4]
    counts += [4, 4, 3, 3, 7, 7, 7, 7]
    counts += [1, 1, 15, 15, 7, 7, 15, 15, 1, 1]
    whole = pl.BlockSpec(memory_space=pltpu.VMEM)
    hbm = pl.BlockSpec(memory_space=pl.ANY)
    projected, grad_features, gk, gp = pl.pallas_call(
        lambda *refs: kernel(scale, *refs),
        out_shape=(
            jax.ShapeDtypeStruct((32, 64, 1024), BF),
            jax.ShapeDtypeStruct((64, 128, 128), BF),
            jax.ShapeDtypeStruct((2, 36, 16, 128), F32),
            jax.ShapeDtypeStruct((32, 512), F32),
        ),
        in_specs=[hbm, whole, whole, hbm],
        out_specs=(hbm, hbm, whole, whole),
        scratch_shapes=[
            vm(64, 128, 128),
            vm(1040, 128, dtype=F32),
            vm(66, 64, 512),
            vm(66, 64, 512),
            vm(32, 64, 512, dtype=F32),
            vm(32, 64, 512),
            vm(512, 2048),
            vm(32, 64, 512, dtype=F32),
            vm(32, 64, 1024),
            vm(4, 4, 2, 32, 512),
            vm(512, 1024),
            vm(1536, 256),
            vm(1536, 256),
            vm(32, 64, 1024),
            vm(64, 128, 128),
            vm(256, 4096),
            vm(3, 256, 512, dtype=F32),
            vm(4, 4, 2, 32, 512),
            vm(4, 4, 32, 512),
            vm(4, 4, 32, 512),
            vm(4, 4, 32, 512),
            vm(4, 2, 16, 512),
            vm(8, 16, 512),
            vm(16, 512),
            vm(8, 16, 512),
            vm(2, 36, 16, 128),
            vm(36, 16, 128),
            vm(16, 3, 16, 128),
            vm(16, 3, 16, 128),
            vm(3, 16, 128),
            vm(8, 3, 16, 128),
            vm(16, 3, 16, 128),
            vm(16, 3, 16, 128),
        ]
        + [dma((n,)) for n in counts],
        compiler_params=pltpu.CompilerParams(
            collective_id=0, has_side_effects=True, vmem_limit_bytes=60 * 1024 * 1024
        ),
    )(features[0], kernel_one, proj_weight, upstream[0])
    return (
        projected[None],
        grad_features[None],
        jnp.transpose(gk.reshape(3, 3, 128, 128), (0, 1, 3, 2)),
        gp.T,
    )


def solution(mesh):
    placed = (P("batch", "tm", None, None), P(), P(None, "tm"), P("batch", "tm", None, None))
    return jax.shard_map(
        body,
        mesh=mesh,
        in_specs=placed,
        out_specs=(P("batch", "tm", None, None), P("batch", "tm", None, None), P(), P(None, "tm")),
        check_vma=False,
    )
```

```python
import math

import jax
import jax.numpy as jnp
from jax import lax
from jax.experimental import pallas as pl
from jax.experimental.pallas import tpu as pltpu
from jax.sharding import PartitionSpec as P

BF = jnp.bfloat16
F32 = jnp.float32
MESH = pl.DeviceIdType.MESH
EARLY = 4


def dot(a, b):
    return jnp.dot(a, b, preferred_element_type=F32)


def place(dst, i, block):
    base = i * 512
    zero = jnp.zeros((128, 128), BF)
    dst[base : base + 128, 0:128] = block(1)
    dst[base : base + 128, 128:256] = block(0)
    dst[base + 128 : base + 256, 0:128] = block(2)
    dst[base + 128 : base + 256, 128:256] = block(1)
    dst[base + 256 : base + 384, 0:128] = block(0)
    dst[base + 256 : base + 384, 128:256] = zero
    dst[base + 384 : base + 512, 0:128] = zero
    dst[base + 384 : base + 512, 128:256] = block(2)


def kernel(
    scale, feat, kern, pwt, up, proj_out, gf_out, gk_out, gp_out,
    st, x4, xta, xtb, y4c, y4w, sl, pk, pkt, gh, wt, wn, wf, wb,
    gps, r0, s1, r1, s2, r2, s3, r3, r4,
    k0, ra, sb, rb, sc, rc, kd, ke,
    in_sem,
    hx_s, hx_r, hy_s, hy_r, wz_s, wz_r, wy_s, wy_r, wc_s, wc_r,
    g0_s, g0_r, g1_s, g1_r, g2_s, g2_r, g3_s, g3_r, g4_s, g4_r,
    ka_s, ka_r, kb_s, kb_r, kc_s, kc_r, kd_s, kd_r, ke_s, ke_r,
):
    tm = lax.axis_index("tm")
    bt = lax.axis_index("batch")
    core, zh, y = tm % 2, (tm // 2) % 4, tm // 8
    x, zl = bt // 2, bt % 2
    z = zh * 2 + zl
    xy = x * 4 + y

    def device(cx, cy, cz, cc):
        return {"tm": (cy * 4 + cz // 2) * 2 + cc, "batch": cx * 2 + cz % 2}

    def remote(src, dst, ssem, rsem, dev):
        return pltpu.make_async_remote_copy(
            src_ref=src, dst_ref=dst, send_sem=ssem, recv_sem=rsem,
            device_id=dev, device_id_type=MESH,
        )

    partner = device(x, y, z, 1 - core)
    left = {"tm": (tm + 31) % 32, "batch": bt}
    right = {"tm": (tm + 1) % 32, "batch": bt}
    side = 2 * zl - 1

    def y_peer(d):
        return device(x, (y + d) % 4, z, core)

    def z_peer(d):
        return device(x, y, (z + d) % 8, core)

    def b_peer(d):
        return {"tm": tm, "batch": (bt + d) % 8}

    def xy_peer(d):
        return device((x + d // 4) % 4, (y + d % 4) % 4, z, core)

    def x_peer(d):
        return device((x + d) % 4, y, z, core)

    barrier = pltpu.get_barrier_semaphore()
    greet = [partner, left, right]
    greet += [z_peer(d) for d in range(1, 8)]
    greet += [b_peer(d) for d in range(1, 8)]
    greet += [xy_peer(d) for d in range(1, 16)]
    for dev in greet:
        pl.semaphore_signal(barrier, inc=1, device_id=dev, device_id_type=MESH)

    fx, ub = gf_out, proj_out
    feat_in = pltpu.make_async_copy(feat, fx, in_sem.at[0])
    up_in = pltpu.make_async_copy(up, ub, in_sem.at[1])
    feat_in.start()
    up_in.start()

    wt[y, zh, core] = pwt[...]
    for i in range(3):
        place(wf, i, lambda j: kern[i, j])

    row = lax.broadcasted_iota(jnp.int32, (512, 128), 0) % 64

    feat_in.wait()

    @pl.loop(0, 8)
    def _(k):
        st[8:1032, :] = fx[pl.ds(k * 8, 8)].reshape(1024, 128).astype(F32)
        at = pl.ds(k * 8 + 1, 8)
        x4[at, :, 0:128] = st[pl.ds(8, 512, stride=2), :].astype(BF).reshape(8, 64, 128)
        x4[at, :, 128:256] = st[pl.ds(9, 512, stride=2), :].astype(BF).reshape(8, 64, 128)
        low = jnp.where(row == 0, 0.0, st[pl.ds(7, 512, stride=2), :])
        x4[at, :, 256:384] = low.astype(BF).reshape(8, 64, 128)
        high = jnp.where(row == 63, 0.0, st[pl.ds(10, 512, stride=2), :])
        x4[at, :, 384:512] = high.astype(BF).reshape(8, 64, 128)

    def forward(k):
        t0 = k * 8
        lhs = jnp.concatenate([x4[pl.ds(t0 + i, 8)].reshape(512, 512) for i in range(3)], axis=1)
        pre = dot(lhs, wf[...])
        here = x4[pl.ds(t0 + 1, 8), :, 0:256].reshape(512, 256).astype(F32)
        sig = 0.5 * jnp.tanh(0.5 * pre) + 0.5
        act = pre * sig
        slope = (sig + act * (1.0 - sig)).reshape(4, 2, 64, 256)
        hidden = (here + act).astype(BF).reshape(4, 2, 64, 256)
        at = pl.ds(k * 4, 4)
        both = jnp.concatenate([hidden[:, 0], hidden[:, 1]], axis=-1)
        pk[at] = both
        sl[at, :, 0:256] = slope[:, 0]
        sl[at, :, 256:512] = slope[:, 1]
        pkt[:, pl.ds(pl.multiple_of(k * 256, 256), 256)] = both.reshape(256, 512).T

    @pl.loop(1, EARLY)
    def _(k):
        forward(k)

    pl.semaphore_wait(barrier, len(greet))

    wz = [
        remote(
            wt.at[y, zh, core], wt.at[y, zh, core], wz_s.at[d - 1], wz_r.at[d - 1],
            device(x, y, (z + side * d + 8) % 8, core),
        )
        for d in range(1, 4)
    ]
    for copy in wz:
        copy.start()
    hx = [
        remote(x4.at[1], x4.at[65], hx_s.at[0], hx_r.at[0], left),
        remote(x4.at[64], x4.at[0], hx_s.at[1], hx_r.at[1], right),
    ]
    for copy in hx:
        copy.start()

    @pl.loop(EARLY, 7)
    def _(k):
        forward(k)

    for copy in hx:
        copy.wait()

    @pl.when(tm == 0)
    def _():
        x4[0] = jnp.zeros((64, 512), BF)

    @pl.when(tm == 31)
    def _():
        x4[65] = jnp.zeros((64, 512), BF)

    forward(0)
    forward(7)

    @pl.loop(0, 8)
    def _(k):
        xtb[:, pl.ds(pl.multiple_of(k * 512, 512), 512)] = x4[pl.ds(k * 8 + 1, 8)].reshape(512, 512).T

    for copy in wz:
        copy.wait()
    wy = {
        d: remote(wt.at[y, :, core], wt.at[y, :, core], wy_s.at[d - 1], wy_r.at[d - 1], y_peer(d))
        for d in (1, 3, 2)
    }
    for copy in wy.values():
        copy.start()

    wc = {
        e: remote(
            wt.at[(y + 4 - e) % 4, :, core], wt.at[(y + 4 - e) % 4, :, core],
            wc_s.at[e], wc_r.at[e], partner,
        )
        for e in range(4)
    }

    wc[0].start()

    up_in.wait()
    g0 = [remote(gps.at[1 - core, :, n], r0.at[:, n], g0_s.at[n], g0_r.at[n], partner) for n in range(4)]
    for n in range(4):
        part = dot(pkt[...], ub[:, :, n * 256 : n * 256 + 256].reshape(2048, 256))
        part = part.astype(BF).T.reshape(4, 2, 32, 512)
        for c in range(2):
            for q in range(4):
                gps[c, q, n] = part[:, c, :, q * 128 : q * 128 + 128]
        g0[n].start()

    @pl.loop(0, 8)
    def _(k):
        xta[:, pl.ds(pl.multiple_of(k * 512, 512), 512)] = x4[pl.ds(k * 8, 8)].reshape(512, 512).T

    xta[:, 4096:4224] = x4[64:66].reshape(128, 512).T

    for copy in g0:
        copy.wait()
    s1[...] = (gps[core].astype(F32) + r0[...].astype(F32)).astype(BF)
    g1 = [
        remote(s1.at[(x + d) % 4], r1.at[x], g1_s.at[d - 1], g1_r.at[d - 1], x_peer(d)) for d in (1, 2, 3)
    ]
    for copy in g1:
        copy.start()
    r1[x] = s1[x]

    for e in (1, 3):
        wy[e].wait()
        wc[e].start()
    for e in (0, 1, 3):
        wc[e].wait()

    near = [y, (y + 1) % 4, (y + 3) % 4]
    far = (y + 2) % 4

    def filters(k, n):
        cols = pl.ds(pl.multiple_of(n * 256, 256), 256)
        return ub[pl.ds(k * 8, 8), :, cols].reshape(512, 256)

    @pl.loop(0, 4)
    def _(k):
        lhs = jnp.concatenate([filters(k, n) for n in near], axis=1)
        rhs = jnp.concatenate([wt[n].reshape(256, 512) for n in near], axis=0)
        gh[pl.ds(k * 8, 8)] = dot(lhs, rhs).reshape(8, 64, 512)

    wy[2].wait()
    wc[2].start()
    wc[2].wait()

    def grads(k):
        at = pl.ds(k * 8, 8)
        gp = gh[at].reshape(512, 512) + dot(filters(k, far), wt[far].reshape(256, 512))
        gh[at] = gp.reshape(8, 64, 512)
        g = (gp * sl[at].reshape(512, 512)).astype(BF).reshape(8, 64, 512)
        for t in range(8):
            for p in range(2):
                y4c[k * 16 + 1 + 2 * t + p] = g[t, :, p * 256 : p * 256 + 256]

    @pl.loop(0, 4)
    def _(k):
        grads(k)

    hy = [
        remote(y4c.at[1], y4c.at[65], hy_s.at[0], hy_r.at[0], left),
        remote(y4c.at[64], y4c.at[0], hy_s.at[1], hy_r.at[1], right),
    ]
    for copy in hy:
        copy.start()

    for i in range(3):
        rows = (xta[:, 0:4096], xtb[...], xta[:, 128:4224])[i]
        full = dot(rows, y4c[1:65].reshape(4096, 256))
        at = [[full[128 * n : 128 * n + 128, 128 * q : 128 * q + 128] for q in range(2)] for n in range(4)]
        parts = (at[0][1] + at[2][0], at[0][0] + at[1][1], at[1][0] + at[3][1])
        for j in range(3):
            block = parts[j].astype(BF).reshape(8, 16, 128)
            n = (i * 3 + j) * 8
            if n < 36 < n + 8:
                k0[0, n:36] = block[: 36 - n]
                k0[1, 0 : n - 28] = block[36 - n :]
            else:
                k0[n // 36, n % 36 : n % 36 + 8] = block
    ka = remote(k0.at[1 - core], ra, ka_s.at[0], ka_r.at[0], partner)
    ka.start()

    for copy in g1:
        copy.wait()
    total = r1[0].astype(F32)
    for n in range(1, 4):
        total = total + r1[n].astype(F32)
    s2[...] = total.astype(BF)
    g2 = [
        remote(s2.at[(y + d) % 4], r2.at[y], g2_s.at[d - 1], g2_r.at[d - 1], y_peer(d)) for d in (1, 2, 3)
    ]

    ka.wait()
    sb[0:12] = (k0[core].astype(F32) + ra[...].astype(F32)).astype(BF).reshape(12, 3, 16, 128)
    sb[12:16] = jnp.zeros((4, 3, 16, 128), BF)
    kb = []
    for d in range(1, 16):
        owner = ((x + d // 4) % 4) * 4 + (y + d % 4) % 4
        kb.append(remote(sb.at[owner], rb.at[xy], kb_s.at[d - 1], kb_r.at[d - 1], xy_peer(d)))
    for copy in kb:
        copy.start()
    for copy in g2:
        copy.start()
    rb[xy] = sb[xy]
    r2[y] = s2[y]

    row3 = lax.broadcasted_iota(jnp.int32, (8, 64, 128), 1)

    def widen(at, n):
        c = y4c[at].astype(F32)
        y4w[at, :, 0:128] = jnp.where(row3[:n] == 0, 0.0, pltpu.roll(c[:, :, 128:256], 1, 1)).astype(BF)
        y4w[at, :, 128:256] = jnp.where(row3[:n] == 63, 0.0, pltpu.roll(c[:, :, 0:128], 63, 1)).astype(BF)

    def backward(k):
        t0 = k * 8
        lhs = []
        for i in range(3):
            lhs.append(y4c[pl.ds(t0 + i, 8)].reshape(512, 256))
            lhs.append(y4w[pl.ds(t0 + i, 8)].reshape(512, 256))
        out = dot(jnp.concatenate(lhs, axis=1), wb[...])
        h = gh[pl.ds(k * 4, 4)]
        out = out + jnp.concatenate(
            [h[t, :, p * 256 : p * 256 + 256] for t in range(4) for p in range(2)], axis=0
        )
        st[pl.ds(8, 512, stride=2), :] = out[:, 0:128]
        st[pl.ds(9, 512, stride=2), :] = out[:, 128:256]
        gf_out[pl.ds(t0, 8)] = st[8:1032, :].astype(BF).reshape(8, 128, 128)

    def project(k):
        proj_out[pl.ds(k * 8, 8)] = (
            dot(pk[pl.ds(k * 8, 8)].reshape(512, 512), wn[...]).astype(BF).reshape(8, 64, 1024)
        )

    @pl.loop(0, 8)
    def _(k):
        widen(pl.ds(k * 8 + 1, 8), 8)

    for i in range(3):
        place(wb, i, lambda j: kern[2 - i, 2 - j].T)

    @pl.loop(1, 4)
    def _(k):
        backward(k)

    for copy in kb:
        copy.wait()
    total = rb[0].astype(F32)
    for n in range(1, 16):
        total = total + rb[n].astype(F32)
    sc[...] = total.astype(BF)
    kc = [remote(sc, rc.at[z], kc_s.at[d - 1], kc_r.at[d - 1], z_peer(d)) for d in range(1, 8)]
    for copy in kc:
        copy.start()
    rc[z] = sc[...]

    for copy in g2:
        copy.wait()
    total = r2[0].astype(F32)
    for n in range(1, 4):
        total = total + r2[n].astype(F32)
    s3[...] = total.astype(BF).reshape(4, 2, 16, 128)
    g3 = []
    for d in range(1, 8):
        zd = (z + d) % 8
        g3.append(remote(s3.at[zd // 2, zd % 2], r3.at[z], g3_s.at[d - 1], g3_r.at[d - 1], z_peer(d)))
    for copy in g3:
        copy.start()
    r3[z] = s3[zh, zl]

    for copy in hy:
        copy.wait()

    @pl.when(tm == 0)
    def _():
        y4c[0] = jnp.zeros((64, 256), BF)

    @pl.when(tm == 31)
    def _():
        y4c[65] = jnp.zeros((64, 256), BF)

    widen(pl.ds(0, 1), 1)
    widen(pl.ds(65, 1), 1)
    backward(0)

    @pl.loop(4, 8)
    def _(k):
        backward(k)

    for copy in kc:
        copy.wait()
    total = rc[0].astype(F32)
    for zz in range(1, 8):
        total = total + rc[zz].astype(F32)
    kd[xy] = total.astype(BF)
    kdc = [
        remote(kd.at[xy], kd.at[xy], kd_s.at[d - 1], kd_r.at[d - 1], xy_peer(d)) for d in range(1, 16)
    ]
    for copy in kdc:
        copy.start()

    for copy in g3:
        copy.wait()
    total = r3[0].astype(F32)
    for n in range(1, 8):
        total = total + r3[n].astype(F32)
    r4[bt] = total * scale
    g4 = [remote(r4.at[bt], r4.at[bt], g4_s.at[d - 1], g4_r.at[d - 1], b_peer(d)) for d in range(1, 8)]
    for copy in g4:
        copy.start()

    for yy in range(4):
        wn[:, yy * 256 : (yy + 1) * 256] = wt[yy].reshape(256, 512).T

    @pl.loop(0, 3)
    def _(k):
        project(k)

    for copy in kdc:
        copy.wait()
    kec = remote(kd, ke, ke_s.at[0], ke_r.at[0], partner)
    kec.start()

    project(3)
    for copy in g4:
        copy.wait()
    for n in range(8):
        q, half = n // 2, n % 2
        gp_out[half * 16 : half * 16 + 16, q * 128 : q * 128 + 128] = r4[n]

    gk_out[core] = kd[0:12].astype(F32).reshape(36, 16, 128) * scale
    kec.wait()
    gk_out[1 - core] = ke[0:12].astype(F32).reshape(36, 16, 128) * scale


def vm(*shape, dtype=BF):
    return pltpu.VMEM(shape, dtype)


def write_out(p_in, f_in, k_in, g_in, p_out, f_out, k_out, g_out, sem):
    pairs = [(p_in.at[n * 4 : n * 4 + 4], p_out.at[n * 4 : n * 4 + 4]) for n in range(8)]
    pairs += [(f_in.at[n * 16 : n * 16 + 16], f_out.at[n * 16 : n * 16 + 16]) for n in range(4)]
    pairs += [(k_in, k_out), (g_in, g_out)]
    copies = [pltpu.make_async_copy(a, b, sem.at[n]) for n, (a, b) in enumerate(pairs)]
    for copy in copies:
        copy.start()
    for copy in copies:
        copy.wait()


def body(features, kernel_one, proj_weight, upstream):
    scale = 1.0 / math.sqrt(8 * 2048 * 128)
    dma = pltpu.SemaphoreType.DMA
    counts = [2]
    counts += [2, 2, 2, 2, 3, 3, 3, 3, 4, 4]
    counts += [4, 4, 3, 3, 3, 3, 7, 7, 7, 7]
    counts += [1, 1, 15, 15, 7, 7, 15, 15, 1, 1]
    whole = pl.BlockSpec(memory_space=pltpu.VMEM)
    hbm = pl.BlockSpec(memory_space=pl.ANY)
    projected, grad_features, gk, gp = pl.pallas_call(
        lambda *refs: kernel(scale, *refs),
        out_shape=(
            vm(32, 64, 1024),
            vm(64, 128, 128),
            vm(2, 36, 16, 128, dtype=F32),
            vm(32, 512, dtype=F32),
        ),
        in_specs=[hbm, whole, whole, hbm],
        out_specs=(whole, whole, whole, whole),
        scratch_shapes=[
            vm(1040, 128, dtype=F32),
            vm(66, 64, 512),
            vm(512, 4224),
            vm(512, 4096),
            vm(66, 64, 256),
            vm(66, 64, 256),
            vm(32, 64, 512, dtype=F32),
            vm(32, 64, 512),
            vm(512, 2048),
            vm(32, 64, 512, dtype=F32),
            vm(4, 4, 2, 32, 512),
            vm(512, 1024),
            vm(1536, 256),
            vm(1536, 256),
            vm(2, 4, 4, 4, 32, 128),
            vm(4, 4, 4, 32, 128),
            vm(4, 4, 4, 32, 128),
            vm(4, 4, 4, 32, 128),
            vm(4, 4, 32, 128),
            vm(4, 4, 32, 128),
            vm(4, 2, 16, 128),
            vm(8, 16, 128),
            vm(8, 16, 128, dtype=F32),
            vm(2, 36, 16, 128),
            vm(36, 16, 128),
            vm(16, 3, 16, 128),
            vm(16, 3, 16, 128),
            vm(3, 16, 128),
            vm(8, 3, 16, 128),
            vm(16, 3, 16, 128),
            vm(16, 3, 16, 128),
        ]
        + [dma((n,)) for n in counts],
        compiler_params=pltpu.CompilerParams(
            collective_id=0, has_side_effects=True, vmem_limit_bytes=52 * 1024 * 1024
        ),
    )(features[0], kernel_one, proj_weight.T, upstream[0])
    results = (projected, grad_features, gk, gp)
    projected, grad_features, gk, gp = pl.pallas_call(
        write_out,
        out_shape=tuple(jax.ShapeDtypeStruct(r.shape, r.dtype) for r in results),
        in_specs=[hbm] * 4,
        out_specs=(hbm,) * 4,
        scratch_shapes=[dma((14,))],
        compiler_params=pltpu.CompilerParams(vmem_limit_bytes=1024 * 1024),
    )(*[pltpu.with_memory_space_constraint(r, pltpu.VMEM) for r in results])
    return projected[None], grad_features[None], gk.reshape(3, 3, 128, 128), gp.T


def solution(mesh):
    placed = (P("batch", "tm", None, None), P(), P(None, "tm"), P("batch", "tm", None, None))
    return jax.shard_map(
        body,
        mesh=mesh,
        in_specs=placed,
        out_specs=(P("batch", "tm", None, None), P("batch", "tm", None, None), P(), P(None, "tm")),
        check_vma=False,
    )
```

```python
import math

import jax
import jax.numpy as jnp
from jax import lax
from jax.experimental import pallas as pl
from jax.experimental.pallas import tpu as pltpu
from jax.sharding import PartitionSpec as P

BF = jnp.bfloat16
F32 = jnp.float32
MESH = pl.DeviceIdType.MESH
EARLY = 2


def dot(a, b):
    return jnp.dot(a, b, preferred_element_type=F32)


def place(dst, i, block):
    base = i * 512
    zero = jnp.zeros((128, 128), BF)
    dst[base : base + 128, 0:128] = block(1)
    dst[base : base + 128, 128:256] = block(0)
    dst[base + 128 : base + 256, 0:128] = block(2)
    dst[base + 128 : base + 256, 128:256] = block(1)
    dst[base + 256 : base + 384, 0:128] = block(0)
    dst[base + 256 : base + 384, 128:256] = zero
    dst[base + 384 : base + 512, 0:128] = zero
    dst[base + 384 : base + 512, 128:256] = block(2)


def kernel(
    scale, feat, kern_in, pwt, up, proj_out, gf_out, gk_out, gp_out,
    kern, st, fh, x4, xta, xtb, y4c, y4w, sl, pk, pkt, gh, wt, wn, wf, wb,
    gps, r0, s1, r1, s2, r2, s3, r3, r4,
    k0, ra, sb, rb, sc, rc, kd, ke,
    in_sem,
    hx_s, hx_r, hy_s, hy_r, wz_s, wz_r, wy_s, wy_r, wc_s, wc_r,
    g0_s, g0_r, g1_s, g1_r, g2_s, g2_r, g3_s, g3_r, g4_s, g4_r,
    ka_s, ka_r, kb_s, kb_r, kc_s, kc_r, kd_s, kd_r, ke_s, ke_r,
):
    tm = lax.axis_index("tm")
    bt = lax.axis_index("batch")
    core, zh, y = tm % 2, (tm // 2) % 4, tm // 8
    x, zl = bt // 2, bt % 2
    z = zh * 2 + zl
    xy = x * 4 + y

    def device(cx, cy, cz, cc):
        return {"tm": (cy * 4 + cz // 2) * 2 + cc, "batch": cx * 2 + cz % 2}

    def remote(src, dst, ssem, rsem, dev):
        return pltpu.make_async_remote_copy(
            src_ref=src, dst_ref=dst, send_sem=ssem, recv_sem=rsem,
            device_id=dev, device_id_type=MESH,
        )

    partner = device(x, y, z, 1 - core)
    left = {"tm": (tm + 31) % 32, "batch": bt}
    right = {"tm": (tm + 1) % 32, "batch": bt}
    side = 2 * zl - 1

    def y_peer(d):
        return device(x, (y + d) % 4, z, core)

    def z_peer(d):
        return device(x, y, (z + d) % 8, core)

    def b_peer(d):
        return {"tm": tm, "batch": (bt + d) % 8}

    def xy_peer(d):
        return device((x + d // 4) % 4, (y + d % 4) % 4, z, core)

    def x_peer(d):
        return device((x + d) % 4, y, z, core)

    barrier = pltpu.get_barrier_semaphore()
    greet = [partner, left, right]
    greet += [z_peer(d) for d in range(1, 8)]
    greet += [b_peer(d) for d in range(1, 8)]
    greet += [xy_peer(d) for d in range(1, 16)]
    for dev in greet:
        pl.semaphore_signal(barrier, inc=1, device_id=dev, device_id_type=MESH)

    fx, ub = gf_out, proj_out
    feat_in = [
        pltpu.make_async_copy(
            feat.at[n * 16 : n * 16 + 16], fx.at[n * 16 : n * 16 + 16], in_sem.at[n]
        )
        for n in range(4)
    ]
    up_in = [
        pltpu.make_async_copy(up.at[n * 8 : n * 8 + 8], ub.at[n * 8 : n * 8 + 8], in_sem.at[4 + n])
        for n in range(4)
    ]
    small_in = [
        pltpu.make_async_copy(kern_in, kern, in_sem.at[8]),
        pltpu.make_async_copy(pwt, wt.at[y, zh, core], in_sem.at[9]),
    ]
    for copy in small_in + feat_in:
        copy.start()
    for copy in small_in:
        copy.wait()

    for i in range(3):
        place(wf, i, lambda j: kern[i, j])

    def build(src, at, frames):
        count = frames * 64
        row = lax.broadcasted_iota(jnp.int32, (count, 128), 0) % 64
        st[8 : 8 + frames * 128, :] = src.reshape(frames * 128, 128).astype(F32)
        shape = (frames, 64, 128)
        x4[at, :, 0:128] = st[pl.ds(8, count, stride=2), :].astype(BF).reshape(shape)
        x4[at, :, 128:256] = st[pl.ds(9, count, stride=2), :].astype(BF).reshape(shape)
        low = jnp.where(row == 0, 0.0, st[pl.ds(7, count, stride=2), :])
        x4[at, :, 256:384] = low.astype(BF).reshape(shape)
        high = jnp.where(row == 63, 0.0, st[pl.ds(10, count, stride=2), :])
        x4[at, :, 384:512] = high.astype(BF).reshape(shape)

    for copy in feat_in:
        copy.wait()
    for copy in up_in:
        copy.start()

    @pl.loop(0, 8)
    def _(k):
        build(fx[pl.ds(k * 8, 8)], pl.ds(k * 8 + 1, 8), 8)

    def forward(k):
        t0 = k * 8
        lhs = jnp.concatenate([x4[pl.ds(t0 + i, 8)].reshape(512, 512) for i in range(3)], axis=1)
        pre = dot(lhs, wf[...])
        here = x4[pl.ds(t0 + 1, 8), :, 0:256].reshape(512, 256).astype(F32)
        sig = 0.5 * jnp.tanh(0.5 * pre) + 0.5
        act = pre * sig
        slope = (sig + act * (1.0 - sig)).reshape(4, 2, 64, 256)
        hidden = (here + act).astype(BF).reshape(4, 2, 64, 256)
        at = pl.ds(k * 4, 4)
        both = jnp.concatenate([hidden[:, 0], hidden[:, 1]], axis=-1)
        pk[at] = both
        sl[at, :, 0:256] = slope[:, 0]
        sl[at, :, 256:512] = slope[:, 1]
        pkt[:, pl.ds(pl.multiple_of(k * 256, 256), 256)] = both.reshape(256, 512).T

    @pl.loop(1, EARLY)
    def _(k):
        forward(k)

    pl.semaphore_wait(barrier, len(greet))

    wz = [
        remote(
            wt.at[y, zh, core], wt.at[y, zh, core], wz_s.at[d - 1], wz_r.at[d - 1],
            device(x, y, (z + side * d + 8) % 8, core),
        )
        for d in range(1, 4)
    ]
    turn = [zh, (zh + side + 4) % 4, (zh - side + 4) % 4, (zh + 2) % 4]
    wy = {
        (n, d): remote(
            wt.at[y, turn[n], core], wt.at[y, turn[n], core],
            wy_s.at[n * 4 + d], wy_r.at[n * 4 + d], y_peer(d),
        )
        for n in range(4)
        for d in (1, 3, 2)
    }

    def along_y(n):
        if n > 0:
            wz[n - 1].wait()
        for d in (1, 3, 2):
            wy[n, d].start()

    for copy in wz:
        copy.start()
    along_y(0)
    hx = [
        remote(fx.at[0], fh.at[1], hx_s.at[0], hx_r.at[0], left),
        remote(fx.at[63], fh.at[0], hx_s.at[1], hx_r.at[1], right),
    ]

    for copy in hx:
        copy.start()

    @pl.loop(EARLY, 7)
    def _(k):
        forward(k)

    along_y(1)

    @pl.loop(0, 8)
    def _(k):
        xtb[:, pl.ds(pl.multiple_of(k * 512, 512), 512)] = x4[pl.ds(k * 8 + 1, 8)].reshape(512, 512).T

    along_y(2)

    @pl.loop(1, 5)
    def _(k):
        xta[:, pl.ds(pl.multiple_of(k * 512, 512), 512)] = x4[pl.ds(k * 8, 8)].reshape(512, 512).T

    along_y(3)
    wc = {
        e: remote(
            wt.at[(y + 4 - e) % 4, :, core], wt.at[(y + 4 - e) % 4, :, core],
            wc_s.at[e], wc_r.at[e], partner,
        )
        for e in range(4)
    }
    wc[0].start()
    for copy in hx:
        copy.wait()

    @pl.when(tm == 0)
    def _():
        fh[0] = jnp.zeros((128, 128), BF)

    @pl.when(tm == 31)
    def _():
        fh[1] = jnp.zeros((128, 128), BF)

    build(fh[0:1], pl.ds(0, 1), 1)
    build(fh[1:2], pl.ds(65, 1), 1)
    forward(0)
    forward(7)

    for copy in up_in:
        copy.wait()
    g0 = [remote(gps.at[1 - core, :, n], r0.at[:, n], g0_s.at[n], g0_r.at[n], partner) for n in range(4)]
    g1 = {
        (n, d): remote(
            s1.at[(x + d) % 4, n], r1.at[x, n], g1_s.at[n * 4 + d], g1_r.at[n * 4 + d], x_peer(d)
        )
        for n in range(4)
        for d in (1, 3, 2)
    }

    def core_sum(n):
        g0[n].wait()
        s1[:, n] = (gps[core, :, n].astype(F32) + r0[:, n].astype(F32)).astype(BF)
        for d in (1, 3, 2):
            g1[n, d].start()
        r1[x, n] = s1[x, n]

    for n in range(4):
        part = dot(pkt[...], ub[:, :, n * 256 : n * 256 + 256].reshape(2048, 256))
        part = part.astype(BF).T.reshape(4, 2, 32, 512)
        for c in range(2):
            for q in range(4):
                gps[c, q, n] = part[:, c, :, q * 128 : q * 128 + 128]
        g0[n].start()
        if n > 1:
            core_sum(n - 2)

    for e in (1, 3, 2):
        for n in range(4):
            wy[n, e].wait()
        wc[e].start()
    core_sum(2)
    core_sum(3)

    @pl.loop(5, 8)
    def _(k):
        xta[:, pl.ds(pl.multiple_of(k * 512, 512), 512)] = x4[pl.ds(k * 8, 8)].reshape(512, 512).T

    xta[:, 0:512] = x4[0:8].reshape(512, 512).T
    xta[:, 4096:4224] = x4[64:66].reshape(128, 512).T

    for copy in wc.values():
        copy.wait()

    @pl.loop(0, 4, unroll=True)
    def _(k):
        at = pl.ds(k * 8, 8)
        gp = dot(ub[at].reshape(512, 1024), wt[...].reshape(1024, 512))
        gh[at] = gp.reshape(8, 64, 512)
        g = (gp * sl[at].reshape(512, 512)).astype(BF).reshape(8, 64, 512)
        for t in range(8):
            for p in range(2):
                y4c[k * 16 + 1 + 2 * t + p] = g[t, :, p * 256 : p * 256 + 256]

    hy = [
        remote(y4c.at[1], y4c.at[65], hy_s.at[0], hy_r.at[0], left),
        remote(y4c.at[64], y4c.at[0], hy_s.at[1], hy_r.at[1], right),
    ]
    for copy in hy:
        copy.start()

    for i in range(3):
        rows = (xta[:, 0:4096], xtb[...], xta[:, 128:4224])[i]
        full = dot(rows, y4c[1:65].reshape(4096, 256))
        at = [[full[128 * n : 128 * n + 128, 128 * q : 128 * q + 128] for q in range(2)] for n in range(4)]
        parts = (at[0][1] + at[2][0], at[0][0] + at[1][1], at[1][0] + at[3][1])
        for j in range(3):
            block = parts[j].astype(BF).reshape(8, 16, 128)
            n = (i * 3 + j) * 8
            if n < 36 < n + 8:
                k0[0, n:36] = block[: 36 - n]
                k0[1, 0 : n - 28] = block[36 - n :]
            else:
                k0[n // 36, n % 36 : n % 36 + 8] = block
    ka = remote(k0.at[1 - core], ra, ka_s.at[0], ka_r.at[0], partner)
    ka.start()

    for copy in g1.values():
        copy.wait()
    total = r1[0].astype(F32)
    for n in range(1, 4):
        total = total + r1[n].astype(F32)
    s2[...] = total.astype(BF)
    g2 = [
        remote(s2.at[(y + d) % 4], r2.at[y], g2_s.at[d - 1], g2_r.at[d - 1], y_peer(d)) for d in (1, 2, 3)
    ]
    for copy in g2:
        copy.start()
    r2[y] = s2[y]

    ka.wait()
    sb[0:12] = (k0[core].astype(F32) + ra[...].astype(F32)).astype(BF).reshape(12, 3, 16, 128)
    sb[12:16] = jnp.zeros((4, 3, 16, 128), BF)
    kb = []
    for d in range(1, 16):
        owner = ((x + d // 4) % 4) * 4 + (y + d % 4) % 4
        kb.append(remote(sb.at[owner], rb.at[xy], kb_s.at[d - 1], kb_r.at[d - 1], xy_peer(d)))
    for copy in kb:
        copy.start()
    rb[xy] = sb[xy]

    row3 = lax.broadcasted_iota(jnp.int32, (8, 64, 128), 1)

    def widen(at, n):
        c = y4c[at].astype(F32)
        y4w[at, :, 0:128] = jnp.where(row3[:n] == 0, 0.0, pltpu.roll(c[:, :, 128:256], 1, 1)).astype(BF)
        y4w[at, :, 128:256] = jnp.where(row3[:n] == 63, 0.0, pltpu.roll(c[:, :, 0:128], 63, 1)).astype(BF)

    def backward(k):
        t0 = k * 8
        lhs = []
        for i in range(3):
            lhs.append(y4c[pl.ds(t0 + i, 8)].reshape(512, 256))
            lhs.append(y4w[pl.ds(t0 + i, 8)].reshape(512, 256))
        out = dot(jnp.concatenate(lhs, axis=1), wb[...])
        h = gh[pl.ds(k * 4, 4)]
        out = out + jnp.concatenate(
            [h[t, :, p * 256 : p * 256 + 256] for t in range(4) for p in range(2)], axis=0
        )
        st[pl.ds(8, 512, stride=2), :] = out[:, 0:128]
        st[pl.ds(9, 512, stride=2), :] = out[:, 128:256]
        gf_out[pl.ds(t0, 8)] = st[8:1032, :].astype(BF).reshape(8, 128, 128)

    def project(k):
        proj_out[pl.ds(k * 8, 8)] = (
            dot(pk[pl.ds(k * 8, 8)].reshape(512, 512), wn[...]).astype(BF).reshape(8, 64, 1024)
        )

    @pl.loop(0, 8)
    def _(k):
        widen(pl.ds(k * 8 + 1, 8), 8)

    for copy in g2:
        copy.wait()
    total = r2[0].astype(F32)
    for n in range(1, 4):
        total = total + r2[n].astype(F32)
    s3[...] = total.astype(BF).reshape(4, 2, 16, 128)
    g3 = []
    for d in range(1, 8):
        zd = (z + d) % 8
        g3.append(remote(s3.at[zd // 2, zd % 2], r3.at[z], g3_s.at[d - 1], g3_r.at[d - 1], z_peer(d)))
    for copy in g3:
        copy.start()
    r3[z] = s3[zh, zl]

    for i in range(3):
        place(wb, i, lambda j: kern[2 - i, 2 - j].T)

    @pl.loop(1, 4)
    def _(k):
        backward(k)

    for copy in kb:
        copy.wait()
    total = rb[0].astype(F32)
    for n in range(1, 16):
        total = total + rb[n].astype(F32)
    sc[...] = total.astype(BF)
    kc = [remote(sc, rc.at[z], kc_s.at[d - 1], kc_r.at[d - 1], z_peer(d)) for d in range(1, 8)]
    for copy in kc:
        copy.start()
    rc[z] = sc[...]

    for copy in hy:
        copy.wait()

    @pl.when(tm == 0)
    def _():
        y4c[0] = jnp.zeros((64, 256), BF)

    @pl.when(tm == 31)
    def _():
        y4c[65] = jnp.zeros((64, 256), BF)

    for copy in g3:
        copy.wait()
    total = r3[0].astype(F32)
    for n in range(1, 8):
        total = total + r3[n].astype(F32)
    r4[bt] = total * scale
    g4 = [remote(r4.at[bt], r4.at[bt], g4_s.at[d - 1], g4_r.at[d - 1], b_peer(d)) for d in range(1, 8)]
    for copy in g4:
        copy.start()

    widen(pl.ds(0, 1), 1)
    widen(pl.ds(65, 1), 1)
    backward(0)

    @pl.loop(4, 8)
    def _(k):
        backward(k)

    for copy in kc:
        copy.wait()
    total = rc[0].astype(F32)
    for zz in range(1, 8):
        total = total + rc[zz].astype(F32)
    kd[xy] = total.astype(BF)
    kdc = [
        remote(kd.at[xy], kd.at[xy], kd_s.at[d - 1], kd_r.at[d - 1], xy_peer(d)) for d in range(1, 16)
    ]
    for copy in kdc:
        copy.start()

    for yy in range(4):
        wn[:, yy * 256 : (yy + 1) * 256] = wt[yy].reshape(256, 512).T

    @pl.loop(0, 3)
    def _(k):
        project(k)

    for copy in kdc:
        copy.wait()
    kec = remote(kd, ke, ke_s.at[0], ke_r.at[0], partner)
    kec.start()

    project(3)
    for copy in g4:
        copy.wait()
    for n in range(8):
        q, half = n // 2, n % 2
        gp_out[half * 16 : half * 16 + 16, q * 128 : q * 128 + 128] = r4[n]

    gk_out[core] = kd[0:12].astype(F32).reshape(36, 16, 128) * scale
    kec.wait()
    gk_out[1 - core] = ke[0:12].astype(F32).reshape(36, 16, 128) * scale


def vm(*shape, dtype=BF):
    return pltpu.VMEM(shape, dtype)


def write_out(p_in, f_in, k_in, g_in, p_out, f_out, k_out, g_out, sem):
    pairs = [(p_in.at[n * 4 : n * 4 + 4], p_out.at[n * 4 : n * 4 + 4]) for n in range(8)]
    pairs += [(f_in.at[n * 16 : n * 16 + 16], f_out.at[n * 16 : n * 16 + 16]) for n in range(4)]
    pairs += [(k_in, k_out), (g_in, g_out)]
    copies = [pltpu.make_async_copy(a, b, sem.at[n]) for n, (a, b) in enumerate(pairs)]
    for copy in copies:
        copy.start()
    for copy in copies:
        copy.wait()


def body(features, kernel_one, proj_weight, upstream):
    scale = 1.0 / math.sqrt(8 * 2048 * 128)
    dma = pltpu.SemaphoreType.DMA
    counts = [10]
    counts += [2, 2, 2, 2, 3, 3, 16, 16, 4, 4]
    counts += [4, 4, 16, 16, 3, 3, 7, 7, 7, 7]
    counts += [1, 1, 15, 15, 7, 7, 15, 15, 1, 1]
    whole = pl.BlockSpec(memory_space=pltpu.VMEM)
    hbm = pl.BlockSpec(memory_space=pl.ANY)
    projected, grad_features, gk, gp = pl.pallas_call(
        lambda *refs: kernel(scale, *refs),
        out_shape=(
            vm(32, 64, 1024),
            vm(64, 128, 128),
            vm(2, 36, 16, 128, dtype=F32),
            vm(32, 512, dtype=F32),
        ),
        in_specs=[hbm] * 4,
        out_specs=(whole, whole, whole, whole),
        scratch_shapes=[
            vm(3, 3, 128, 128),
            vm(1040, 128, dtype=F32),
            vm(2, 128, 128),
            vm(66, 64, 512),
            vm(512, 4224),
            vm(512, 4096),
            vm(66, 64, 256),
            vm(66, 64, 256),
            vm(32, 64, 512, dtype=F32),
            vm(32, 64, 512),
            vm(512, 2048),
            vm(32, 64, 512, dtype=F32),
            vm(4, 4, 2, 32, 512),
            vm(512, 1024),
            vm(1536, 256),
            vm(1536, 256),
            vm(2, 4, 4, 4, 32, 128),
            vm(4, 4, 4, 32, 128),
            vm(4, 4, 4, 32, 128),
            vm(4, 4, 4, 32, 128),
            vm(4, 4, 32, 128),
            vm(4, 4, 32, 128),
            vm(4, 2, 16, 128),
            vm(8, 16, 128),
            vm(8, 16, 128, dtype=F32),
            vm(2, 36, 16, 128),
            vm(36, 16, 128),
            vm(16, 3, 16, 128),
            vm(16, 3, 16, 128),
            vm(3, 16, 128),
            vm(8, 3, 16, 128),
            vm(16, 3, 16, 128),
            vm(16, 3, 16, 128),
        ]
        + [dma((n,)) for n in counts],
        compiler_params=pltpu.CompilerParams(
            collective_id=0, has_side_effects=True, vmem_limit_bytes=52 * 1024 * 1024
        ),
    )(features[0], kernel_one, proj_weight.T, upstream[0])
    results = (projected, grad_features, gk, gp)
    projected, grad_features, gk, gp = pl.pallas_call(
        write_out,
        out_shape=tuple(jax.ShapeDtypeStruct(r.shape, r.dtype) for r in results),
        in_specs=[hbm] * 4,
        out_specs=(hbm,) * 4,
        scratch_shapes=[dma((14,))],
        compiler_params=pltpu.CompilerParams(vmem_limit_bytes=1024 * 1024),
    )(*[pltpu.with_memory_space_constraint(r, pltpu.VMEM) for r in results])
    return projected[None], grad_features[None], gk.reshape(3, 3, 128, 128), gp.T


def solution(mesh):
    placed = (P("batch", "tm", None, None), P(), P(None, "tm"), P("batch", "tm", None, None))
    return jax.shard_map(
        body,
        mesh=mesh,
        in_specs=placed,
        out_specs=(P("batch", "tm", None, None), P("batch", "tm", None, None), P(), P(None, "tm")),
        check_vma=False,
    )
```

```python
import math

import jax
import jax.numpy as jnp
from jax import lax
from jax.experimental import pallas as pl
from jax.experimental.pallas import tpu as pltpu
from jax.sharding import PartitionSpec as P

BF = jnp.bfloat16
F32 = jnp.float32
MESH = pl.DeviceIdType.MESH
EARLY = 2


def dot(a, b):
    return jnp.dot(a, b, preferred_element_type=F32)


def place(dst, i, block):
    base = i * 512
    zero = jnp.zeros((128, 128), BF)
    dst[base : base + 128, 0:128] = block(1)
    dst[base : base + 128, 128:256] = block(0)
    dst[base + 128 : base + 256, 0:128] = block(2)
    dst[base + 128 : base + 256, 128:256] = block(1)
    dst[base + 256 : base + 384, 0:128] = block(0)
    dst[base + 256 : base + 384, 128:256] = zero
    dst[base + 384 : base + 512, 0:128] = zero
    dst[base + 384 : base + 512, 128:256] = block(2)


def kernel(
    scale, feat, kern_in, pwt, up, proj_out, gf_out, gk_out, gp_out,
    kern, st, fh, x4, xta, xtb, y4c, y4w, sl, pk, pkt, gh, wt, wn, wf, wb,
    gps, r0, s1, r1, s2, r2, s3, r3, r4,
    k0, ra, sb, rb, sc, rc, kd, ke,
    in_sem,
    hx_s, hx_r, hy_s, hy_r, wz_s, wz_r, wy_s, wy_r, wc_s, wc_r,
    g0_s, g0_r, g1_s, g1_r, g2_s, g2_r, g3_s, g3_r, g4_s, g4_r,
    ka_s, ka_r, kb_s, kb_r, kc_s, kc_r, kd_s, kd_r, ke_s, ke_r,
):
    tm = lax.axis_index("tm")
    bt = lax.axis_index("batch")
    core, zh, y = tm % 2, (tm // 2) % 4, tm // 8
    x, zl = bt // 2, bt % 2
    z = zh * 2 + zl
    xy = x * 4 + y

    def device(cx, cy, cz, cc):
        return {"tm": (cy * 4 + cz // 2) * 2 + cc, "batch": cx * 2 + cz % 2}

    def remote(src, dst, ssem, rsem, dev):
        return pltpu.make_async_remote_copy(
            src_ref=src, dst_ref=dst, send_sem=ssem, recv_sem=rsem,
            device_id=dev, device_id_type=MESH,
        )

    partner = device(x, y, z, 1 - core)
    left = {"tm": (tm + 31) % 32, "batch": bt}
    right = {"tm": (tm + 1) % 32, "batch": bt}
    side = 2 * zl - 1

    def y_peer(d):
        return device(x, (y + d) % 4, z, core)

    def z_peer(d):
        return device(x, y, (z + d) % 8, core)

    def b_peer(d):
        return {"tm": tm, "batch": (bt + d) % 8}

    def xy_peer(d):
        return device((x + d // 4) % 4, (y + d % 4) % 4, z, core)

    def x_peer(d):
        return device((x + d) % 4, y, z, core)

    barrier = pltpu.get_barrier_semaphore()
    greet = [partner, left, right]
    greet += [z_peer(d) for d in range(1, 8)]
    greet += [b_peer(d) for d in range(1, 8)]
    greet += [xy_peer(d) for d in range(1, 16)]
    for dev in greet:
        pl.semaphore_signal(barrier, inc=1, device_id=dev, device_id_type=MESH)

    fx, ub = gf_out, proj_out
    feat_in = [
        pltpu.make_async_copy(
            feat.at[n * 16 : n * 16 + 16], fx.at[n * 16 : n * 16 + 16], in_sem.at[n]
        )
        for n in range(4)
    ]
    up_in = [
        pltpu.make_async_copy(up.at[n * 8 : n * 8 + 8], ub.at[n * 8 : n * 8 + 8], in_sem.at[4 + n])
        for n in range(4)
    ]
    small_in = [
        pltpu.make_async_copy(kern_in, kern, in_sem.at[8]),
        pltpu.make_async_copy(pwt, wt.at[y, zh, core], in_sem.at[9]),
    ]
    for copy in small_in + feat_in:
        copy.start()
    for copy in small_in:
        copy.wait()

    for i in range(3):
        place(wf, i, lambda j: kern[i, j])

    def build(src, at, frames):
        count = frames * 64
        row = lax.broadcasted_iota(jnp.int32, (count, 128), 0) % 64
        st[8 : 8 + frames * 128, :] = src.reshape(frames * 128, 128).astype(F32)
        shape = (frames, 64, 128)
        x4[at, :, 0:128] = st[pl.ds(8, count, stride=2), :].astype(BF).reshape(shape)
        x4[at, :, 128:256] = st[pl.ds(9, count, stride=2), :].astype(BF).reshape(shape)
        low = jnp.where(row == 0, 0.0, st[pl.ds(7, count, stride=2), :])
        x4[at, :, 256:384] = low.astype(BF).reshape(shape)
        high = jnp.where(row == 63, 0.0, st[pl.ds(10, count, stride=2), :])
        x4[at, :, 384:512] = high.astype(BF).reshape(shape)

    for copy in feat_in:
        copy.wait()
    for copy in up_in:
        copy.start()

    @pl.loop(0, 8)
    def _(k):
        build(fx[pl.ds(k * 8, 8)], pl.ds(k * 8 + 1, 8), 8)

    def forward(k):
        t0 = k * 8
        lhs = jnp.concatenate([x4[pl.ds(t0 + i, 8)].reshape(512, 512) for i in range(3)], axis=1)
        pre = dot(lhs, wf[...])
        here = x4[pl.ds(t0 + 1, 8), :, 0:256].reshape(512, 256).astype(F32)
        sig = 0.5 * jnp.tanh(0.5 * pre) + 0.5
        act = pre * sig
        slope = (sig + act * (1.0 - sig)).reshape(4, 2, 64, 256)
        hidden = (here + act).astype(BF).reshape(4, 2, 64, 256)
        at = pl.ds(k * 4, 4)
        both = jnp.concatenate([hidden[:, 0], hidden[:, 1]], axis=-1)
        pk[at] = both
        sl[at, :, 0:256] = slope[:, 0]
        sl[at, :, 256:512] = slope[:, 1]
        pkt[:, pl.ds(pl.multiple_of(k * 256, 256), 256)] = both.reshape(256, 512).T

    @pl.loop(1, EARLY)
    def _(k):
        forward(k)

    pl.semaphore_wait(barrier, len(greet))

    wz = [
        remote(
            wt.at[y, zh, core], wt.at[y, zh, core], wz_s.at[d - 1], wz_r.at[d - 1],
            device(x, y, (z + side * d + 8) % 8, core),
        )
        for d in range(1, 4)
    ]
    turn = [zh, (zh + side + 4) % 4, (zh - side + 4) % 4, (zh + 2) % 4]
    wy = {
        (n, d): remote(
            wt.at[y, turn[n], core], wt.at[y, turn[n], core],
            wy_s.at[n * 4 + d], wy_r.at[n * 4 + d], y_peer(d),
        )
        for n in range(4)
        for d in (1, 3, 2)
    }

    def along_y(n):
        if n > 0:
            wz[n - 1].wait()
        for d in (1, 3, 2):
            wy[n, d].start()

    for copy in wz:
        copy.start()
    along_y(0)
    hx = [
        remote(fx.at[0], fh.at[1], hx_s.at[0], hx_r.at[0], left),
        remote(fx.at[63], fh.at[0], hx_s.at[1], hx_r.at[1], right),
    ]

    for copy in hx:
        copy.start()

    @pl.loop(EARLY, 7)
    def _(k):
        forward(k)

    along_y(1)

    @pl.loop(0, 8)
    def _(k):
        xtb[:, pl.ds(pl.multiple_of(k * 512, 512), 512)] = x4[pl.ds(k * 8 + 1, 8)].reshape(512, 512).T

    along_y(2)

    @pl.loop(1, 5)
    def _(k):
        xta[:, pl.ds(pl.multiple_of(k * 512, 512), 512)] = x4[pl.ds(k * 8, 8)].reshape(512, 512).T

    along_y(3)
    wc = {
        e: remote(
            wt.at[(y + 4 - e) % 4, :, core], wt.at[(y + 4 - e) % 4, :, core],
            wc_s.at[e], wc_r.at[e], partner,
        )
        for e in range(4)
    }
    wc[0].start()
    for copy in hx:
        copy.wait()

    @pl.when(tm == 0)
    def _():
        fh[0] = jnp.zeros((128, 128), BF)

    @pl.when(tm == 31)
    def _():
        fh[1] = jnp.zeros((128, 128), BF)

    build(fh[0:1], pl.ds(0, 1), 1)
    build(fh[1:2], pl.ds(65, 1), 1)
    forward(0)
    forward(7)

    for copy in up_in:
        copy.wait()
    g0 = [remote(gps.at[1 - core, :, n], r0.at[:, n], g0_s.at[n], g0_r.at[n], partner) for n in range(4)]
    g1 = {
        (n, d): remote(
            s1.at[(x + d) % 4, n], r1.at[x, n], g1_s.at[n * 4 + d], g1_r.at[n * 4 + d], x_peer(d)
        )
        for n in range(4)
        for d in (1, 3, 2)
    }

    def core_sum(n):
        g0[n].wait()
        s1[:, n] = (gps[core, :, n].astype(F32) + r0[:, n].astype(F32)).astype(BF)
        for d in (1, 3, 2):
            g1[n, d].start()
        r1[x, n] = s1[x, n]

    for n in range(4):
        part = dot(pkt[...], ub[:, :, n * 256 : n * 256 + 256].reshape(2048, 256))
        part = part.astype(BF).T.reshape(4, 2, 32, 512)
        for c in range(2):
            for q in range(4):
                gps[c, q, n] = part[:, c, :, q * 128 : q * 128 + 128]
        g0[n].start()
        if n > 1:
            core_sum(n - 2)

    for e in (1, 3, 2):
        for n in range(4):
            wy[n, e].wait()
        wc[e].start()
    core_sum(2)
    core_sum(3)

    @pl.loop(5, 8)
    def _(k):
        xta[:, pl.ds(pl.multiple_of(k * 512, 512), 512)] = x4[pl.ds(k * 8, 8)].reshape(512, 512).T

    xta[:, 0:512] = x4[0:8].reshape(512, 512).T
    xta[:, 4096:4224] = x4[64:66].reshape(128, 512).T

    for copy in wc.values():
        copy.wait()

    @pl.loop(0, 4, unroll=True)
    def _(k):
        at = pl.ds(k * 8, 8)
        gp = dot(ub[at].reshape(512, 1024), wt[...].reshape(1024, 512))
        gh[at] = gp.reshape(8, 64, 512)
        g = (gp * sl[at].reshape(512, 512)).astype(BF).reshape(8, 64, 512)
        for t in range(8):
            for p in range(2):
                y4c[k * 16 + 1 + 2 * t + p] = g[t, :, p * 256 : p * 256 + 256]

    hy = [
        remote(y4c.at[1], y4c.at[65], hy_s.at[0], hy_r.at[0], left),
        remote(y4c.at[64], y4c.at[0], hy_s.at[1], hy_r.at[1], right),
    ]
    for copy in hy:
        copy.start()

    for i in range(3):
        rows = (xta[:, 0:4096], xtb[...], xta[:, 128:4224])[i]
        full = dot(rows, y4c[1:65].reshape(4096, 256))
        at = [[full[128 * n : 128 * n + 128, 128 * q : 128 * q + 128] for q in range(2)] for n in range(4)]
        parts = (at[0][1] + at[2][0], at[0][0] + at[1][1], at[1][0] + at[3][1])
        for j in range(3):
            block = parts[j].astype(BF).reshape(8, 16, 128)
            n = (i * 3 + j) * 8
            if n < 36 < n + 8:
                k0[0, n:36] = block[: 36 - n]
                k0[1, 0 : n - 28] = block[36 - n :]
            else:
                k0[n // 36, n % 36 : n % 36 + 8] = block
    ka = remote(k0.at[1 - core], ra, ka_s.at[0], ka_r.at[0], partner)
    ka.start()

    ka.wait()
    sb[0:12] = (k0[core].astype(F32) + ra[...].astype(F32)).astype(BF).reshape(12, 3, 16, 128)
    sb[12:16] = jnp.zeros((4, 3, 16, 128), BF)
    kb = []
    for d in range(1, 16):
        owner = ((x + d // 4) % 4) * 4 + (y + d % 4) % 4
        kb.append(remote(sb.at[owner], rb.at[xy], kb_s.at[d - 1], kb_r.at[d - 1], xy_peer(d)))
    for copy in kb:
        copy.start()
    rb[xy] = sb[xy]

    for copy in g1.values():
        copy.wait()
    total = r1[0].astype(F32)
    for n in range(1, 4):
        total = total + r1[n].astype(F32)
    s2[...] = total.astype(BF)
    g2 = [
        remote(s2.at[(y + d) % 4], r2.at[y], g2_s.at[d - 1], g2_r.at[d - 1], y_peer(d)) for d in (1, 2, 3)
    ]
    for copy in g2:
        copy.start()
    r2[y] = s2[y]

    row3 = lax.broadcasted_iota(jnp.int32, (8, 64, 128), 1)

    def widen(at, n):
        c = y4c[at].astype(F32)
        y4w[at, :, 0:128] = jnp.where(row3[:n] == 0, 0.0, pltpu.roll(c[:, :, 128:256], 1, 1)).astype(BF)
        y4w[at, :, 128:256] = jnp.where(row3[:n] == 63, 0.0, pltpu.roll(c[:, :, 0:128], 63, 1)).astype(BF)

    def backward(k):
        t0 = k * 8
        lhs = []
        for i in range(3):
            lhs.append(y4c[pl.ds(t0 + i, 8)].reshape(512, 256))
            lhs.append(y4w[pl.ds(t0 + i, 8)].reshape(512, 256))
        out = dot(jnp.concatenate(lhs, axis=1), wb[...])
        h = gh[pl.ds(k * 4, 4)]
        out = out + jnp.concatenate(
            [h[t, :, p * 256 : p * 256 + 256] for t in range(4) for p in range(2)], axis=0
        )
        st[pl.ds(8, 512, stride=2), :] = out[:, 0:128]
        st[pl.ds(9, 512, stride=2), :] = out[:, 128:256]
        gf_out[pl.ds(t0, 8)] = st[8:1032, :].astype(BF).reshape(8, 128, 128)

    def project(k):
        proj_out[pl.ds(k * 8, 8)] = (
            dot(pk[pl.ds(k * 8, 8)].reshape(512, 512), wn[...]).astype(BF).reshape(8, 64, 1024)
        )

    @pl.loop(0, 8)
    def _(k):
        widen(pl.ds(k * 8 + 1, 8), 8)

    for i in range(3):
        place(wb, i, lambda j: kern[2 - i, 2 - j].T)

    @pl.loop(1, 3)
    def _(k):
        backward(k)

    for copy in kb:
        copy.wait()
    total = rb[0].astype(F32)
    for n in range(1, 16):
        total = total + rb[n].astype(F32)
    sc[...] = total.astype(BF)
    kc = [remote(sc, rc.at[z], kc_s.at[d - 1], kc_r.at[d - 1], z_peer(d)) for d in range(1, 8)]
    for copy in kc:
        copy.start()
    rc[z] = sc[...]

    for copy in g2:
        copy.wait()
    total = r2[0].astype(F32)
    for n in range(1, 4):
        total = total + r2[n].astype(F32)
    s3[...] = total.astype(BF).reshape(4, 2, 16, 128)
    g3 = []
    for d in range(1, 8):
        zd = (z + d) % 8
        g3.append(remote(s3.at[zd // 2, zd % 2], r3.at[z], g3_s.at[d - 1], g3_r.at[d - 1], z_peer(d)))
    for copy in g3:
        copy.start()
    r3[z] = s3[zh, zl]

    for copy in hy:
        copy.wait()

    @pl.when(tm == 0)
    def _():
        y4c[0] = jnp.zeros((64, 256), BF)

    @pl.when(tm == 31)
    def _():
        y4c[65] = jnp.zeros((64, 256), BF)

    widen(pl.ds(0, 1), 1)
    widen(pl.ds(65, 1), 1)
    backward(0)

    @pl.loop(3, 6)
    def _(k):
        backward(k)

    for copy in kc:
        copy.wait()
    total = rc[0].astype(F32)
    for zz in range(1, 8):
        total = total + rc[zz].astype(F32)
    kd[xy] = total.astype(BF)
    kdc = [
        remote(kd.at[xy], kd.at[xy], kd_s.at[d - 1], kd_r.at[d - 1], xy_peer(d)) for d in range(1, 16)
    ]
    for copy in kdc:
        copy.start()

    for copy in g3:
        copy.wait()
    total = r3[0].astype(F32)
    for n in range(1, 8):
        total = total + r3[n].astype(F32)
    r4[bt] = total * scale
    g4 = [remote(r4.at[bt], r4.at[bt], g4_s.at[d - 1], g4_r.at[d - 1], b_peer(d)) for d in range(1, 8)]
    for copy in g4:
        copy.start()

    @pl.loop(6, 8)
    def _(k):
        backward(k)

    for yy in range(4):
        wn[:, yy * 256 : (yy + 1) * 256] = wt[yy].reshape(256, 512).T

    @pl.loop(0, 3)
    def _(k):
        project(k)

    for copy in kdc:
        copy.wait()
    kec = remote(kd, ke, ke_s.at[0], ke_r.at[0], partner)
    kec.start()

    project(3)
    for copy in g4:
        copy.wait()
    for n in range(8):
        q, half = n // 2, n % 2
        gp_out[half * 16 : half * 16 + 16, q * 128 : q * 128 + 128] = r4[n]

    gk_out[core] = kd[0:12].astype(F32).reshape(36, 16, 128) * scale
    kec.wait()
    gk_out[1 - core] = ke[0:12].astype(F32).reshape(36, 16, 128) * scale


def vm(*shape, dtype=BF):
    return pltpu.VMEM(shape, dtype)


def write_out(p_in, f_in, k_in, g_in, p_out, f_out, k_out, g_out, sem):
    pairs = [(p_in.at[n * 4 : n * 4 + 4], p_out.at[n * 4 : n * 4 + 4]) for n in range(8)]
    pairs += [(f_in.at[n * 16 : n * 16 + 16], f_out.at[n * 16 : n * 16 + 16]) for n in range(4)]
    pairs += [(k_in, k_out), (g_in, g_out)]
    copies = [pltpu.make_async_copy(a, b, sem.at[n]) for n, (a, b) in enumerate(pairs)]
    for copy in copies:
        copy.start()
    for copy in copies:
        copy.wait()


def body(features, kernel_one, proj_weight, upstream):
    scale = 1.0 / math.sqrt(8 * 2048 * 128)
    dma = pltpu.SemaphoreType.DMA
    counts = [10]
    counts += [2, 2, 2, 2, 3, 3, 16, 16, 4, 4]
    counts += [4, 4, 16, 16, 3, 3, 7, 7, 7, 7]
    counts += [1, 1, 15, 15, 7, 7, 15, 15, 1, 1]
    whole = pl.BlockSpec(memory_space=pltpu.VMEM)
    hbm = pl.BlockSpec(memory_space=pl.ANY)
    projected, grad_features, gk, gp = pl.pallas_call(
        lambda *refs: kernel(scale, *refs),
        out_shape=(
            vm(32, 64, 1024),
            vm(64, 128, 128),
            vm(2, 36, 16, 128, dtype=F32),
            vm(32, 512, dtype=F32),
        ),
        in_specs=[hbm] * 4,
        out_specs=(whole, whole, whole, whole),
        scratch_shapes=[
            vm(3, 3, 128, 128),
            vm(1040, 128, dtype=F32),
            vm(2, 128, 128),
            vm(66, 64, 512),
            vm(512, 4224),
            vm(512, 4096),
            vm(66, 64, 256),
            vm(66, 64, 256),
            vm(32, 64, 512, dtype=F32),
            vm(32, 64, 512),
            vm(512, 2048),
            vm(32, 64, 512, dtype=F32),
            vm(4, 4, 2, 32, 512),
            vm(512, 1024),
            vm(1536, 256),
            vm(1536, 256),
            vm(2, 4, 4, 4, 32, 128),
            vm(4, 4, 4, 32, 128),
            vm(4, 4, 4, 32, 128),
            vm(4, 4, 4, 32, 128),
            vm(4, 4, 32, 128),
            vm(4, 4, 32, 128),
            vm(4, 2, 16, 128),
            vm(8, 16, 128),
            vm(8, 16, 128, dtype=F32),
            vm(2, 36, 16, 128),
            vm(36, 16, 128),
            vm(16, 3, 16, 128),
            vm(16, 3, 16, 128),
            vm(3, 16, 128),
            vm(8, 3, 16, 128),
            vm(16, 3, 16, 128),
            vm(16, 3, 16, 128),
        ]
        + [dma((n,)) for n in counts],
        compiler_params=pltpu.CompilerParams(
            collective_id=0, has_side_effects=True, vmem_limit_bytes=52 * 1024 * 1024
        ),
    )(features[0], kernel_one, proj_weight.T, upstream[0])
    results = (projected, grad_features, gk, gp)
    projected, grad_features, gk, gp = pl.pallas_call(
        write_out,
        out_shape=tuple(jax.ShapeDtypeStruct(r.shape, r.dtype) for r in results),
        in_specs=[hbm] * 4,
        out_specs=(hbm,) * 4,
        scratch_shapes=[dma((14,))],
        compiler_params=pltpu.CompilerParams(vmem_limit_bytes=1024 * 1024),
    )(*[pltpu.with_memory_space_constraint(r, pltpu.VMEM) for r in results])
    return projected[None], grad_features[None], gk.reshape(3, 3, 128, 128), gp.T


def solution(mesh):
    placed = (P("batch", "tm", None, None), P(), P(None, "tm"), P("batch", "tm", None, None))
    return jax.shard_map(
        body,
        mesh=mesh,
        in_specs=placed,
        out_specs=(P("batch", "tm", None, None), P("batch", "tm", None, None), P(), P(None, "tm")),
        check_vma=False,
    )
```
